32 devices in a mesh: groups: 2 (over x), mp: 8 (over z, y), member: 2 (over core).
Axes of the slice: x: 2, y: 2, z: 4, core: 2. Of those that a mesh axis runs over, the one named last changes fastest.
Arguments:
- latent: bfloat16 [2, 2048, 1024], P('member', ('groups', 'mp')), parts along dimension 1, may hold values from -8 to 8
- project_in: bfloat16 [1024, 3072], replicated, may hold values from -4 to 4
- project_out: bfloat16 [1024, 1024], replicated, may hold values from -0.75 to 0.75
- decoder_weight: bfloat16 [1024, 1024], replicated, may hold values from -0.1875 to 0.1875
- readout_weight: bfloat16 [100, 1024], replicated, may hold values from -0.1875 to 0.1875
- variable_weight: float32 [100], replicated, may hold values from 0.2 to 2
- area_weight: float32 [4096], P(('groups', 'mp')), parts along dimension 0, may hold values from 0.1 to 6
- current_state: float32 [100, 4096], P(None, ('groups', 'mp')), parts along dimension 1, may hold values from -6 to 6
- target: float32 [100, 4096], P(None, ('groups', 'mp')), parts along dimension 1, may hold values from -6 to 6
- block_table: int32 [16, 3, 2], P('groups'), parts along dimension 0, may hold values from 0 to 7, as said below
- edge_source: int32 [3, 4096], P(None, ('groups', 'mp')), parts along dimension 1, may hold values from 0 to 95, as said below
- edge_weight: float32 [3, 4096], P(None, ('groups', 'mp')), parts along dimension 1, may hold values from 0.2 to 0.6
Outputs:
- mean_loss: float32 [2], P('groups'), parts along dimension 0
- latent_grad: float32 [2, 2048, 1024], P('member', ('groups', 'mp')), parts along dimension 1
- decoder_grad: float32 [2048, 1024], P(('groups', 'mp')), parts along dimension 0
The draws below stay inside these ranges and needn't reach their ends.
There are 2 independent parts, one for each index of `groups`. The reference program is written for one: setup_inputs(seed, part) draws one part's arguments, and reference() takes and returns one part's arrays. A program takes and returns all parts, laid end to end along the dimension named above; an argument that names none is the same for every part. Nothing has to cross between parts.
Inputs may be any that keep to these rules, and one draw needn't show every extreme that they name: block_table[t, j, :] lists 2 distinct blocks (each of 16 latent rows, 8 to a device) of index t + j - 1 of mp that tile t receives; entries naming an index outside 0 to 7 are never read. edge_source[k, g] = j * 2 * 16 + c * 16 + r names row r of block block_table[t, j, c] of index t + j - 1 of mp, for g on tile t; that index lies within 0 to 7.
All inputs are finite; a program needn't handle non-finite values.
Results may differ from the reference program's by a relative error of at most 0.013.
Values may be sent and summed in bfloat16 or wider, within the bound.
A program may use at most 64 MiB of HBM per device.

```python
import math
import jax
import jax.numpy as jnp
from jax import lax

D = 1024
HEADS = 16
VARS = 100
NEIGHBOURS = 3
BLOCK_ROWS = 16
SLOTS = 2
LAT_DEV = 128
GRID_DEV = 256
MEMBERS = 2
LATENT = 1024
GRID = 2048
BLOCKS = 8
N_MP = 8


def route_tables(key):
    count_key, first_key, stride_key = jax.random.split(key, 3)
    counts = jax.random.randint(count_key, (N_MP, 3), 1, SLOTS + 1)
    counts = counts.at[:, 1].set(SLOTS)
    counts = counts.at[0, 0].set(0)
    counts = counts.at[N_MP - 1, 2].set(0)
    first_block = jax.random.randint(first_key, (N_MP, 3, 1), 0, BLOCKS)
    stride = jax.random.randint(stride_key, (N_MP, 3, 1), 1, (BLOCKS - 1) // (SLOTS - 1) + 1)
    table = (first_block + jnp.arange(SLOTS)[None, None, :] * stride) % BLOCKS
    return (counts.astype(jnp.int32), table.astype(jnp.int32))


def draw_block_table(key, part):
    counts, table = route_tables(key)
    return table.astype(jnp.int32)


def draw_edge_source(key, part):
    counts, table = route_tables(key)
    key = jax.random.fold_in(key, 53)
    pick_key, row_key = jax.random.split(key)
    live = jnp.sum(counts, axis=1)
    pick = jax.random.randint(pick_key, (NEIGHBOURS, N_MP, GRID_DEV), 0, live[None, :, None])
    ending = jnp.cumsum(counts, axis=1)
    starting = ending - counts
    source = jnp.sum((pick[..., None] >= ending[None, :, None, :]).astype(jnp.int32), axis=-1)
    chosen = (source[..., None] == jnp.arange(3)[None, None, None, :]).astype(jnp.int32)
    slot = pick - jnp.sum(chosen * starting[None, :, None, :], axis=-1)
    row = jax.random.randint(row_key, (NEIGHBOURS, N_MP, GRID_DEV), 0, BLOCK_ROWS)
    position = source * SLOTS * BLOCK_ROWS + slot * BLOCK_ROWS + row
    position = position.at[0, 1, 0].set(3 * SLOTS * BLOCK_ROWS - 1)
    position = position.at[1, 1, 0].set(0)
    return position.reshape(NEIGHBOURS, GRID).astype(jnp.int32)


def draw_area_weight(key, part):
    key = jax.random.fold_in(key, 37)
    position_share = (jnp.arange(GRID, dtype=jnp.float32) + 0.5) / GRID
    rough = jnp.exp(jax.random.uniform(key, (GRID,), jnp.float32, 0.0, math.log(3.0)))
    values = (0.5 + position_share) * rough
    return values.astype(jnp.float32)


def draw_latent(key, part):
    key = jax.random.fold_in(key, 11)
    base_key = jax.random.fold_in(key, 0)
    base = jax.random.normal(base_key, (MEMBERS, LATENT, D), jnp.float32)
    values = base
    return jnp.clip(values, -8.0, 8.0).astype(jnp.bfloat16)


def draw_project_in(key, part):
    key = jax.random.fold_in(key, 23)
    query_key, key_key, value_key = jax.random.split(key, 3)
    scale = D ** (-0.5)
    query_part = jax.random.normal(query_key, (D, D), jnp.float32) * scale
    key_part = jax.random.normal(key_key, (D, D), jnp.float32) * scale
    value_part = jax.random.normal(value_key, (D, D), jnp.float32) * scale
    return jnp.clip(jnp.concatenate([query_part, key_part, value_part], axis=1), -4.0, 4.0).astype(jnp.bfloat16)


def shard_levels(stream_key, dims, shards, least, top_value):
    def one(axis_at, shards_of):
        heights = jax.random.uniform(jax.random.fold_in(jax.random.fold_in(stream_key, 6), axis_at), (shards_of,), jnp.float32, least / len(shards), top_value / len(shards))
        return jnp.repeat(jnp.exp(heights), dims[axis_at] // shards_of).reshape((-1,) + (1,) * (len(dims) - axis_at - 1))

    loudness = one(*shards[0])
    for cut in shards[1:]:
        loudness = loudness * one(*cut)
    return loudness


def noise(own_key, dims, width, most, pieces=(), held_as=jnp.bfloat16):
    result = jax.random.normal(own_key, dims, jnp.float32) * width
    if len(pieces) > 0:
        result = shard_levels(own_key, dims, pieces, -0.22, 0.18) * result
    return jnp.clip(result, min=-most, max=most).astype(held_as)


def setup_inputs(seed: int = 0, part: int = 0) -> dict:
    keys = jax.random.split(jax.random.key(seed), 13)
    part_splits = jax.random.split(jax.random.fold_in(keys[12], part), 13)
    return {
        "latent": draw_latent(jax.random.fold_in(jax.random.fold_in(keys[12], part), 71), part),
        "project_in": draw_project_in(jax.random.fold_in(keys[12], 71), part),
        "project_out": noise(keys[2], (D, D), (D // 16) ** -0.5, 0.75),
        "decoder_weight": noise(keys[3], (D, D), D ** -0.5, 0.1875),
        "readout_weight": noise(keys[4], (VARS, D), D ** -0.5, 0.1875),
        "variable_weight": jnp.clip(jnp.exp(jax.random.uniform(keys[5], (VARS,), jnp.float32, math.log(0.2), math.log(2.0))), 0.2, 2.0),
        "area_weight": draw_area_weight(jax.random.fold_in(jax.random.fold_in(keys[12], part), 71), part),
        "current_state": noise(part_splits[7], (VARS, GRID), 1.0, 6.0, ((1, 8),), jnp.float32),
        "target": noise(part_splits[8], (VARS, GRID), 1.0, 6.0, ((1, 8),), jnp.float32),
        "block_table": draw_block_table(jax.random.fold_in(jax.random.fold_in(keys[12], part), 71), part),
        "edge_source": draw_edge_source(jax.random.fold_in(jax.random.fold_in(keys[12], part), 71), part),
        "edge_weight": jnp.clip(0.2 + 0.400000021 * jax.random.uniform(part_splits[11], (NEIGHBOURS, GRID), jnp.float32) ** shard_levels(part_splits[11], (NEIGHBOURS, GRID), ((1, 8),), -0.2, 0.2), 0.2, 0.6),
    }


EPSILON = 1e-05
SMOOTH = 0.01
SMOOTH_ROOT = 0.1
MASKED = -1e+30

def layer_norm(values):
    row_mean = lax.optimization_barrier(jnp.mean(values, axis=-1, keepdims=True))
    centred = values - row_mean
    inverse = lax.rsqrt(lax.optimization_barrier(jnp.mean(centred * centred, axis=-1, keepdims=True)) + EPSILON)
    return (centred * inverse, inverse)

def attend(queries, keys_vals, first_query, first_key, total_rows):
    query_rows, model_width = queries.shape
    key_rows = keys_vals.shape[0]
    head_size = model_width // HEADS
    query_heads = queries.reshape(query_rows, HEADS, head_size).astype(jnp.float32)
    key_heads = keys_vals[:, :model_width].reshape(key_rows, HEADS, head_size).astype(jnp.float32)
    value_heads = keys_vals[:, model_width:].reshape(key_rows, HEADS, head_size).astype(jnp.float32)
    scores = jnp.einsum('qhd,khd->hqk', query_heads, key_heads) * head_size ** (-0.5)
    query_place = first_query + jnp.arange(query_rows, dtype=jnp.int32)
    key_place = first_key + jnp.arange(key_rows, dtype=jnp.int32)
    allowed = (jnp.abs(query_place[:, None] - key_place[None, :]) <= LAT_DEV) & (key_place[None, :] >= 0) & (key_place[None, :] < total_rows)
    scores = jnp.where(allowed[None], scores, MASKED)
    largest = lax.optimization_barrier(jnp.max(scores, axis=-1, keepdims=True))
    powers = jnp.exp(scores - largest)
    softmax_weights = (powers / lax.optimization_barrier(jnp.sum(powers, axis=-1, keepdims=True))).astype(jnp.bfloat16)
    context = jnp.einsum('hqk,khd->qhd', softmax_weights.astype(jnp.float32), value_heads)
    return context.reshape(query_rows, model_width).astype(jnp.bfloat16)

def process(tokens, project_in, project_out):
    model_width = tokens.shape[1]
    normed = layer_norm(tokens.astype(jnp.float32))[0].astype(jnp.bfloat16)
    projected = jnp.dot(normed, project_in, preferred_element_type=jnp.float32).astype(jnp.bfloat16)
    queries = projected[:, :model_width]
    keys_vals = projected[:, model_width:]
    padded = jnp.pad(keys_vals, ((LAT_DEV, LAT_DEV), (0, 0)))

    def one_block(block_index):
        first_row = block_index * LAT_DEV
        block_queries = lax.dynamic_slice_in_dim(queries, first_row, LAT_DEV, 0)
        block_keys = lax.dynamic_slice_in_dim(padded, first_row, 3 * LAT_DEV, 0)
        return attend(block_queries, block_keys, first_row, first_row - LAT_DEV, LATENT)
    context = lax.map(one_block, jnp.arange(N_MP, dtype=jnp.int32)).reshape(LATENT, model_width)
    mixed = jnp.dot(context, project_out, preferred_element_type=jnp.float32)
    return (tokens.astype(jnp.float32) + mixed).astype(jnp.bfloat16)

def decode_forward(features, row_index, edge_weight, decoder_weight, readout_weight, current_state):
    aggregate = jnp.zeros((row_index.shape[1], features.shape[1]), jnp.float32)
    for neighbour in range(row_index.shape[0]):
        aggregate = aggregate + edge_weight[neighbour][:, None] * features[row_index[neighbour]].astype(jnp.float32)
    unit_rows, inverse = layer_norm(aggregate)
    unit_rounded = unit_rows.astype(jnp.bfloat16)
    pre_gelu = jnp.dot(unit_rounded, decoder_weight, preferred_element_type=jnp.float32)
    hidden = jax.nn.gelu(pre_gelu).astype(jnp.bfloat16)
    increment = lax.dot_general(readout_weight, hidden, (((1,), (1,)), ((), ())), preferred_element_type=jnp.float32)
    return (current_state + increment, (unit_rows, inverse, unit_rounded, pre_gelu))

def decode_backward(grad_prediction, stored_parts, row_index, edge_weight, decoder_weight, readout_weight, row_total):
    unit_rows, inverse, unit_rounded, pre_gelu = stored_parts
    grad_hidden = lax.dot_general(grad_prediction, readout_weight, (((0,), (0,)), ((), ())), preferred_element_type=jnp.float32)
    gelu_value, gelu_back = jax.vjp(jax.nn.gelu, pre_gelu)
    grad_pre = gelu_back(grad_hidden)[0].astype(jnp.bfloat16)
    grad_weight = lax.dot_general(unit_rounded, grad_pre, (((0,), (0,)), ((), ())), preferred_element_type=jnp.float32)
    grad_unit = lax.dot_general(grad_pre, decoder_weight, (((1,), (1,)), ((), ())), preferred_element_type=jnp.float32)
    grad_aggregate = inverse * (grad_unit - lax.optimization_barrier(jnp.mean(grad_unit, axis=-1, keepdims=True)) - unit_rows * lax.optimization_barrier(jnp.mean(grad_unit * unit_rows, axis=-1, keepdims=True)))
    grad_features = jnp.zeros((row_total, grad_aggregate.shape[1]), jnp.float32)
    for neighbour in range(row_index.shape[0]):
        grad_features = grad_features.at[row_index[neighbour]].add(edge_weight[neighbour][:, None] * grad_aggregate)
    return (grad_features, grad_weight)

def smoothed(difference):
    return jnp.sqrt(difference * difference + SMOOTH) - SMOOTH_ROOT

def smooth_slope(difference):
    return difference / jnp.sqrt(difference * difference + SMOOTH)

def crps_parts(every, own, target, loss_weights, member_count):
    spread = own[None] - every
    objective = loss_weights * (smoothed(own - target) / member_count - lax.optimization_barrier(jnp.sum(smoothed(spread), axis=0)) / (2 * member_count * (member_count - 1)))
    gradient = loss_weights * (smooth_slope(own - target) / member_count - lax.optimization_barrier(jnp.sum(smooth_slope(spread), axis=0)) / (member_count * (member_count - 1)))
    return (jnp.sum(objective), gradient.astype(jnp.bfloat16))

def reference(latent, project_in, project_out, decoder_weight, readout_weight, variable_weight, area_weight, current_state, target, block_table, edge_source, edge_weight):
    model_width = latent.shape[2]
    latent_out = jnp.stack([process(latent[member], project_in, project_out) for member in range(MEMBERS)])
    slot_rows = SLOTS * BLOCK_ROWS

    def one_tile(carry, tile):
        objective_sum, grad_latent, grad_weight = carry
        table_row = lax.dynamic_index_in_dim(block_table, tile, 0, keepdims=False)
        source_index = tile + jnp.arange(3, dtype=jnp.int32) - 1
        row_map = (source_index[:, None, None] * LAT_DEV + table_row[:, :, None] * BLOCK_ROWS + jnp.arange(BLOCK_ROWS, dtype=jnp.int32)[None, None, :]).reshape(3 * slot_rows)
        row_map = jnp.clip(row_map, 0, LATENT - 1).astype(jnp.int32)
        first_point = tile * GRID_DEV
        row_index = row_map[lax.dynamic_slice_in_dim(edge_source, first_point, GRID_DEV, 1)]
        tile_weights = lax.dynamic_slice_in_dim(edge_weight, first_point, GRID_DEV, 1)
        tile_state = lax.dynamic_slice_in_dim(current_state, first_point, GRID_DEV, 1)
        tile_target = lax.dynamic_slice_in_dim(target, first_point, GRID_DEV, 1)
        tile_area = lax.dynamic_slice_in_dim(area_weight, first_point, GRID_DEV, 0)
        loss_weights = variable_weight[:, None] * tile_area[None, :]
        forwards = [decode_forward(latent_out[member], row_index, tile_weights, decoder_weight, readout_weight, tile_state) for member in range(MEMBERS)]
        every = jnp.stack([forwards[member][0] for member in range(MEMBERS)])
        tile_grads = []
        for member in range(MEMBERS):
            part_sum, grad_prediction = crps_parts(every, every[member], tile_target, loss_weights, MEMBERS)
            objective_sum = objective_sum + part_sum
            grad_features, grad_member = decode_backward(grad_prediction, forwards[member][1], row_index, tile_weights, decoder_weight, readout_weight, LATENT)
            grad_weight = grad_weight + grad_member
            tile_grads.append(lax.optimization_barrier(grad_features.astype(jnp.bfloat16)).astype(jnp.float32))
        grad_latent = grad_latent + jnp.stack(tile_grads)
        return ((objective_sum, grad_latent, grad_weight), None)
    start = (jnp.zeros((), jnp.float32), jnp.zeros((MEMBERS, LATENT, model_width), jnp.float32), jnp.zeros((model_width, model_width), jnp.float32))
    final, unused = lax.scan(one_tile, start, jnp.arange(N_MP, dtype=jnp.int32))
    objective_sum, grad_latent, grad_weight = final
    return (jnp.reshape(objective_sum / GRID, (1,)), grad_latent, grad_weight)
```

```python
import functools

import jax
import jax.numpy as jnp
from jax import lax
from jax.experimental import pallas as pl
from jax.experimental.pallas import tpu as pltpu
from jax.sharding import PartitionSpec as P

HEADS = 16
BLOCK_ROWS = 16
SLOTS = 2
LAT_DEV = 128
PIECES = 4
VAR_PAD = 104
READ_PAD = 128

EPSILON = 1e-05
SMOOTH = 0.01
SMOOTH_ROOT = 0.1
MASKED = -1e30
GELU_SCALE = 0.7978845608028654
GELU_CUBE = 0.044715

MESH = pl.DeviceIdType.MESH
F32 = jnp.float32
BF16 = jnp.bfloat16


def dot(a, b, dims=((1,), (0,))):
    return lax.dot_general(a, b, (dims, ((), ())), preferred_element_type=F32)


def layer_norm(values):
    row_mean = jnp.mean(values, axis=-1, keepdims=True)
    centred = values - row_mean
    inverse = lax.rsqrt(jnp.mean(centred * centred, axis=-1, keepdims=True) + EPSILON)
    return (centred * inverse, inverse)


def kernel(
    count,
    grid_total,
    tokens_hbm,
    in_hbm,
    out_hbm,
    decoder_hbm,
    readout_ref,
    variable_ref,
    area_ref,
    state_ref,
    target_ref,
    table_ref,
    source_ref,
    weight_ref,
    loss_ref,
    latent_grad_ref,
    decoder_grad_ref,
    tok,
    w_in,
    w_out,
    w_dec,
    q_s,
    k_s,
    v_s,
    ctx_s,
    chosen,
    feats,
    unit_s,
    units,
    pre_s,
    slope_s,
    readout_pad,
    state_pad,
    target_pad,
    variable_pad,
    pred_own,
    pred_other,
    loss_own,
    loss_all,
    gpre_s,
    gpre_other,
    grad_send,
    grad_recv,
    y_send,
    y_recv,
    z_send,
    z_recv,
    share_own,
    share_other,
    local_sem,
    halo_sem,
    pass_sem,
    feat_sem,
    pair_sem,
    loss_send_sem,
    loss_recv_sem,
    grad_sem,
    ys_sem,
    yr_sem,
    zs_sem,
    zr_sem,
):
    group = lax.axis_index("groups")
    idx = lax.axis_index("mp")
    member = lax.axis_index("member")
    other = 1 - member
    depth = count // 2
    parity = lax.rem(idx, 2)
    level = lax.div(idx, 2)
    partner = idx + 1 - 2 * parity
    width = tok.shape[2]
    half = width // 2
    share_rows = width // count
    piece = LAT_DEV // PIECES
    arrive = 2 - 2 * parity
    far = 2 - arrive
    onward = idx + 2 - 4 * parity
    origin = idx - 2 + 4 * parity
    has_onward = (onward >= 0) & (onward < count)
    has_origin = (origin >= 0) & (origin < count)
    has_low = idx > 0
    has_high = idx < count - 1

    def at(place, who):
        return (group, place, who)

    def remote(src, dst, send, recv, place, who):
        return pltpu.make_async_remote_copy(
            src_ref=src,
            dst_ref=dst,
            send_sem=send,
            recv_sem=recv,
            device_id=at(place, who),
            device_id_type=MESH,
        )

    own_copy = pltpu.make_async_copy(tokens_hbm.at[0], tok.at[1], local_sem.at[0])
    own_copy.start()
    in_copies = []
    for part in range(3):
        columns = pl.ds(part * width, width)
        in_copies.append(
            pltpu.make_async_copy(
                in_hbm.at[:, columns], w_in.at[:, columns], local_sem.at[1 + part]
            )
        )
        in_copies[-1].start()
    out_copy = pltpu.make_async_copy(out_hbm, w_out, local_sem.at[4])
    out_copy.start()
    dec_copy = pltpu.make_async_copy(decoder_hbm, w_dec, local_sem.at[5])
    dec_copy.start()

    barrier = pltpu.get_barrier_semaphore()
    for step in range(1, count):
        pl.semaphore_signal(
            barrier,
            inc=1,
            device_id=at(lax.rem(idx + step, count), member),
            device_id_type=MESH,
        )
    pl.semaphore_signal(barrier, inc=1, device_id=at(idx, other), device_id_type=MESH)
    pl.semaphore_wait(barrier, count)

    def halo_copy(c):
        rows = pl.ds(c * piece, piece)
        return remote(
            tokens_hbm.at[0, rows],
            tok.at[far, rows],
            halo_sem.at[0, c],
            halo_sem.at[1, c],
            partner,
            member,
        )

    def pass_copy(c):
        rows = pl.ds(c * piece, piece)
        return remote(
            tok.at[arrive, rows],
            tok.at[far, rows],
            pass_sem.at[0, c],
            pass_sem.at[1, c],
            onward,
            member,
        )

    for c in range(PIECES):
        halo_copy(c).start()

    @pl.when(jnp.logical_not(has_origin))
    def _():
        tok[far] = jnp.zeros((LAT_DEV, width), BF16)

    @pl.when(jnp.logical_not(has_low))
    def _():
        feats[0] = jnp.zeros(feats.shape[1:], BF16)
        grad_recv[0] = jnp.zeros(grad_recv.shape[1:], BF16)

    @pl.when(jnp.logical_not(has_high))
    def _():
        feats[2] = jnp.zeros(feats.shape[1:], BF16)
        grad_recv[2] = jnp.zeros(grad_recv.shape[1:], BF16)

    def relay(c):
        halo_copy(c).wait_recv()

        @pl.when(has_onward)
        def _():
            pass_copy(c).start()

    own_copy.wait()
    normed = layer_norm(tok[1].astype(F32))[0].astype(BF16)
    in_copies[0].wait()
    q_s[...] = (dot(normed, w_in[:, :width]) * (HEADS / width) ** 0.5).astype(BF16)
    relay(0)
    in_copies[1].wait()
    k_s[LAT_DEV : 2 * LAT_DEV] = dot(normed, w_in[:, width : 2 * width]).astype(BF16)
    relay(1)
    in_copies[2].wait()
    v_s[LAT_DEV : 2 * LAT_DEV] = dot(normed, w_in[:, 2 * width :]).astype(BF16)

    readout_pad[...] = jnp.zeros(readout_pad.shape, F32)
    state_pad[...] = jnp.zeros(state_pad.shape, F32)
    target_pad[...] = jnp.zeros(target_pad.shape, F32)
    variable_pad[...] = jnp.zeros(variable_pad.shape, F32)
    variables = readout_ref.shape[0]
    readout_pad[0:variables] = readout_ref[...].astype(F32)
    state_pad[0:variables] = state_ref[...]
    target_pad[0:variables] = target_ref[...]
    variable_pad[0:1, 0:variables] = variable_ref[...]
    relay(2)
    relay(3)

    def keys_values(slot):
        rows = pl.ds(pl.multiple_of(slot * LAT_DEV, LAT_DEV), LAT_DEV)
        halo = layer_norm(tok[slot].astype(F32))[0].astype(BF16)
        k_s[rows] = dot(halo, w_in[:, width : 2 * width]).astype(BF16)
        v_s[rows] = dot(halo, w_in[:, 2 * width :]).astype(BF16)

    keys_values(arrive)

    @pl.when(has_origin)
    def _():
        for c in range(PIECES):
            pass_copy(c).wait_recv()

    keys_values(far)

    query_at = lax.broadcasted_iota(jnp.int32, (LAT_DEV, 3 * LAT_DEV), 0)
    key_at = lax.broadcasted_iota(jnp.int32, (LAT_DEV, 3 * LAT_DEV), 1)
    place = key_at + (idx - 1) * LAT_DEV
    allowed = (
        (key_at >= query_at)
        & (key_at <= query_at + 2 * LAT_DEV)
        & (place >= 0)
        & (place < count * LAT_DEV)
    )
    bias = jnp.where(allowed, 0.0, MASKED)
    bias = jnp.concatenate([bias, bias], axis=0)
    first_head = lax.broadcasted_iota(jnp.int32, (LAT_DEV, 128), 1) < 64
    for pair in range(width // 128):
        columns = slice(pair * 128, (pair + 1) * 128)
        queries = q_s[:, columns].astype(F32)
        queries = jnp.concatenate(
            [jnp.where(first_head, queries, 0.0), jnp.where(first_head, 0.0, queries)], axis=0
        ).astype(BF16)
        scores = dot(queries, k_s[:, columns], ((1,), (1,))) + bias
        powers = jnp.exp(scores - jnp.max(scores, axis=-1, keepdims=True))
        total = jnp.sum(powers, axis=-1, keepdims=True)
        context = dot(powers.astype(BF16), v_s[:, columns]) / total
        ctx_s[:, columns] = jnp.where(
            first_head, context[:LAT_DEV], context[LAT_DEV:]
        ).astype(BF16)

    out_copy.wait()
    mixed = dot(ctx_s[...], w_out[...])
    latent_out = (tok[1].astype(F32) + mixed).astype(BF16)

    below = jnp.maximum(idx - 1, 0)
    above = jnp.minimum(idx + 1, count - 1)
    row_at = lax.broadcasted_iota(jnp.int32, (BLOCK_ROWS, LAT_DEV), 0)
    column_at = lax.broadcasted_iota(jnp.int32, (BLOCK_ROWS, LAT_DEV), 1)
    picks = []
    for tile, j, live in ((below, 2, has_low), (idx, 1, True), (above, 0, has_high)):
        for c in range(SLOTS):
            hit = column_at == row_at + table_ref[tile, j, c] * BLOCK_ROWS
            pick = jnp.where(hit, 1.0, 0.0)
            if live is not True:
                pick = pick * jnp.where(live, 1.0, 0.0)
            picks.append(pick)
    pick = jnp.concatenate(picks, axis=0).astype(BF16)
    slot_rows = SLOTS * BLOCK_ROWS
    chosen_rows = dot(pick, latent_out).astype(BF16)
    for j in range(3):
        chosen[j] = chosen_rows[j * slot_rows : (j + 1) * slot_rows]
    feats[1] = chosen_rows[slot_rows : 2 * slot_rows]

    feat_down = remote(
        chosen.at[0], feats.at[2], feat_sem.at[0], feat_sem.at[1], idx - 1, member
    )
    feat_up = remote(chosen.at[2], feats.at[0], feat_sem.at[2], feat_sem.at[3], idx + 1, member)

    @pl.when(has_low)
    def _():
        feat_down.start()

    @pl.when(has_high)
    def _():
        feat_up.start()

    grid_rows = source_ref.shape[1]
    position = lax.broadcasted_iota(jnp.int32, (3 * slot_rows, grid_rows), 0)
    spread = jnp.zeros((3 * slot_rows, grid_rows), F32)
    for k in range(3):
        spread = spread + jnp.where(
            position == source_ref[k : k + 1, :], weight_ref[k : k + 1, :], 0.0
        )
    spread_high = spread.astype(BF16)
    spread_low = (spread - spread_high.astype(F32)).astype(BF16)
    readout = readout_pad[...].astype(BF16)
    diagonal = lax.broadcasted_iota(jnp.int32, (READ_PAD, 128), 0) == lax.broadcasted_iota(
        jnp.int32, (READ_PAD, 128), 1
    )
    variable = jnp.sum(jnp.where(diagonal, variable_pad[0:1, :], 0.0), axis=1, keepdims=True)
    loss_weights = variable * area_ref[...]

    @pl.when(has_high)
    def _():
        feat_down_in = remote(
            chosen.at[0], feats.at[2], feat_sem.at[0], feat_sem.at[1], idx + 1, member
        )
        feat_down_in.wait_recv()

    @pl.when(has_low)
    def _():
        feat_up_in = remote(
            chosen.at[2], feats.at[0], feat_sem.at[2], feat_sem.at[3], idx - 1, member
        )
        feat_up_in.wait_recv()

    all_rows = feats[...].reshape(3 * slot_rows, width)
    aggregate = dot(
        jnp.concatenate([spread_high, spread_low], axis=0),
        jnp.concatenate([all_rows, all_rows], axis=0),
        ((0,), (0,)),
    )
    unit, inverse = layer_norm(aggregate)
    unit_s[...] = unit
    dec_copy.wait()
    pre = dot(unit.astype(BF16), w_dec[...])
    pre_s[...] = pre
    hidden = (
        0.5 * pre * (1.0 + jnp.tanh(GELU_SCALE * (pre + GELU_CUBE * pre * pre * pre)))
    ).astype(BF16)
    prediction = state_pad[...] + dot(readout, hidden, ((1,), (1,)))
    pred_own[...] = prediction[:VAR_PAD]
    pred_copy = remote(pred_own, pred_other, pair_sem.at[2], pair_sem.at[3], idx, other)
    pred_copy.start()

    units[0] = jnp.transpose(unit_s[...]).astype(BF16)
    unit_copy = remote(units.at[0], units.at[1], pair_sem.at[0], pair_sem.at[1], idx, other)
    unit_copy.start()

    pre = pre_s[...]
    square = pre * pre
    bend = jnp.tanh(GELU_SCALE * (pre + GELU_CUBE * pre * square))
    slope_s[...] = 0.5 * (1.0 + bend) + 0.5 * pre * (1.0 - bend * bend) * (
        GELU_SCALE * (1.0 + 3.0 * GELU_CUBE * square)
    )

    pred_copy.wait_recv()
    mine = pred_own[...]
    theirs = pred_other[...]
    target = target_pad[...][:VAR_PAD]
    weights = loss_weights[:VAR_PAD]
    miss = mine - target
    miss_other = theirs - target
    apart = mine - theirs
    miss_root = jnp.sqrt(miss * miss + SMOOTH)
    other_root = jnp.sqrt(miss_other * miss_other + SMOOTH)
    apart_root = jnp.sqrt(apart * apart + SMOOTH)
    objective = weights * (
        ((miss_root - SMOOTH_ROOT) + (other_root - SMOOTH_ROOT)) * 0.5
        - (apart_root - SMOOTH_ROOT) * 0.5
    )
    terms = jnp.sum(objective.reshape(VAR_PAD // 8, 8, grid_rows), axis=0)
    folded = terms[:, :128]
    for start in range(128, grid_rows, 128):
        folded = folded + terms[:, start : start + 128]
    loss_own[...] = folded
    loss_all[idx] = folded
    grad_prediction = weights * (miss / miss_root * 0.5 - apart / apart_root * 0.5)
    grad_prediction = jnp.concatenate(
        [grad_prediction, jnp.zeros((READ_PAD - VAR_PAD, grid_rows), F32)], axis=0
    ).astype(BF16)

    grad_hidden = dot(grad_prediction, readout, ((0,), (0,)))
    grad_pre = (grad_hidden * slope_s[...]).astype(BF16)
    gpre_s[0] = grad_pre[:, :half]
    gpre_s[1] = grad_pre[:, half:]
    gpre_copy = remote(
        gpre_s.at[other], gpre_other, pair_sem.at[4], pair_sem.at[5], idx, other
    )
    gpre_copy.start()

    def loss_copy(step):
        goal = lax.rem(idx + step, count)
        return remote(
            loss_own,
            loss_all.at[idx],
            loss_send_sem.at[step],
            loss_recv_sem.at[step],
            goal,
            member,
        )

    def loss_in(step):
        start = lax.rem(idx + count - step, count)
        return remote(
            loss_own,
            loss_all.at[start],
            loss_send_sem.at[step],
            loss_recv_sem.at[step],
            start,
            member,
        )

    for step in range(1, count):
        loss_copy(step).start()

    unit_copy.wait_recv()
    gpre_copy.wait_recv()
    grad_here = jnp.concatenate([gpre_s[member], gpre_other[...]], axis=0)

    def weight_rows(chunk):
        rows = pl.ds(pl.multiple_of(chunk * share_rows, share_rows), share_rows)
        return dot(jnp.concatenate([units[0, rows], units[1, rows]], axis=1), grad_here)

    def y_copy(step):
        return remote(
            y_send.at[step], y_recv.at[step], ys_sem.at[step], yr_sem.at[step], partner, member
        )

    def z_copy(step):
        goal = 2 * lax.rem(level + step, depth) + parity
        return remote(
            z_send.at[step], z_recv.at[step], zs_sem.at[step], zr_sem.at[step], goal, member
        )

    def send_partner(i, carry):
        step = lax.rem(i + 1, depth)
        chunk = 2 * lax.rem(level + step, depth) + (1 - parity)
        y_send[step] = weight_rows(chunk).astype(BF16)
        y_copy(step).start()
        return carry

    lax.fori_loop(0, depth, send_partner, 0)

    grad_unit = dot(jnp.concatenate([gpre_s[0], gpre_s[1]], axis=1), w_dec[...], ((1,), (1,)))
    unit = unit_s[...]
    grad_aggregate = inverse * (
        grad_unit
        - jnp.mean(grad_unit, axis=-1, keepdims=True)
        - unit * jnp.mean(grad_unit * unit, axis=-1, keepdims=True)
    )
    rounded = grad_aggregate.astype(BF16)
    tile_grad = (dot(spread_high, rounded) + dot(spread_low, rounded)).astype(BF16)
    grad_send[0] = tile_grad[:slot_rows]
    grad_send[1] = tile_grad[2 * slot_rows :]
    grad_recv[1] = tile_grad[slot_rows : 2 * slot_rows]
    grad_down = remote(
        grad_send.at[0], grad_recv.at[2], grad_sem.at[0], grad_sem.at[1], idx - 1, member
    )
    grad_up = remote(
        grad_send.at[1], grad_recv.at[0], grad_sem.at[2], grad_sem.at[3], idx + 1, member
    )

    @pl.when(has_low)
    def _():
        grad_down.start()

    @pl.when(has_high)
    def _():
        grad_up.start()

    def send_level(i, carry):
        step = i + 1
        chunk = 2 * lax.rem(level + step, depth) + parity
        rows = weight_rows(chunk)
        y_copy(step).wait_recv()
        z_send[step] = (rows + y_recv[step].astype(F32)).astype(BF16)
        z_copy(step).start()
        return carry

    lax.fori_loop(0, depth - 1, send_level, 0)
    share = weight_rows(idx)
    y_copy(0).wait_recv()
    share = share + y_recv[0].astype(F32)

    @pl.when(has_high)
    def _():
        remote(
            grad_send.at[0], grad_recv.at[2], grad_sem.at[0], grad_sem.at[1], idx + 1, member
        ).wait_recv()

    @pl.when(has_low)
    def _():
        remote(
            grad_send.at[1], grad_recv.at[0], grad_sem.at[2], grad_sem.at[3], idx - 1, member
        ).wait_recv()

    latent_grad_ref[0] = dot(
        pick, grad_recv[...].reshape(3 * slot_rows, width), ((0,), (0,))
    )

    for step in range(1, count):
        loss_in(step).wait_recv()
    loss_sum = loss_all[0]
    for step in range(1, count):
        loss_sum = loss_sum + loss_all[step]
    loss_ref[0] = jnp.sum(loss_sum) / grid_total

    for step in range(1, depth):
        z_copy(step).wait_recv()
        share = share + z_recv[step].astype(F32)
    share_own[...] = share.astype(BF16)
    share_copy = remote(share_own, share_other, pair_sem.at[6], pair_sem.at[7], idx, other)
    share_copy.start()
    own_columns = pl.ds(pl.multiple_of(member * half, half), half)
    other_columns = pl.ds(pl.multiple_of(other * half, half), half)
    decoder_grad_ref[:, own_columns] = share_own[...].astype(F32)
    share_copy.wait_recv()
    decoder_grad_ref[:, other_columns] = share_other[...].astype(F32)

    for c in range(PIECES):
        halo_copy(c).wait_send()

    @pl.when(has_onward)
    def _():
        for c in range(PIECES):
            pass_copy(c).wait_send()

    @pl.when(has_low)
    def _():
        feat_down.wait_send()
        grad_down.wait_send()

    @pl.when(has_high)
    def _():
        feat_up.wait_send()
        grad_up.wait_send()

    unit_copy.wait_send()
    pred_copy.wait_send()
    gpre_copy.wait_send()
    share_copy.wait_send()
    for step in range(1, count):
        loss_copy(step).wait_send()
    for step in range(depth):
        y_copy(step).wait_send()
    for step in range(1, depth):
        z_copy(step).wait_send()


def body(
    latent,
    project_in,
    project_out,
    decoder_weight,
    readout_weight,
    variable_weight,
    area_weight,
    current_state,
    target,
    block_table,
    edge_source,
    edge_weight,
):
    count = lax.axis_size("mp")
    width = latent.shape[2]
    half = width // 2
    depth = count // 2
    share_rows = width // count
    grid_rows = edge_source.shape[1]
    slot_rows = SLOTS * BLOCK_ROWS
    hbm = pl.BlockSpec(memory_space=pl.ANY)
    vmem = pl.BlockSpec(memory_space=pltpu.VMEM)
    smem = pl.BlockSpec(memory_space=pltpu.SMEM)
    dma = pltpu.SemaphoreType.DMA
    return pl.pallas_call(
        functools.partial(kernel, count, float(count * grid_rows)),
        out_shape=(
            jax.ShapeDtypeStruct((1,), F32),
            jax.ShapeDtypeStruct((1, LAT_DEV, width), F32),
            jax.ShapeDtypeStruct((share_rows, width), F32),
        ),
        in_specs=[hbm, hbm, hbm, hbm, vmem, vmem, vmem, vmem, vmem, smem, vmem, vmem],
        out_specs=(smem, vmem, vmem),
        scratch_shapes=[
            pltpu.VMEM((3, LAT_DEV, width), BF16),
            pltpu.VMEM((width, 3 * width), BF16),
            pltpu.VMEM((width, width), BF16),
            pltpu.VMEM((width, width), BF16),
            pltpu.VMEM((LAT_DEV, width), BF16),
            pltpu.VMEM((3 * LAT_DEV, width), BF16),
            pltpu.VMEM((3 * LAT_DEV, width), BF16),
            pltpu.VMEM((LAT_DEV, width), BF16),
            pltpu.VMEM((3, slot_rows, width), BF16),
            pltpu.VMEM((3, slot_rows, width), BF16),
            pltpu.VMEM((grid_rows, width), F32),
            pltpu.VMEM((2, width, grid_rows), BF16),
            pltpu.VMEM((grid_rows, width), F32),
            pltpu.VMEM((grid_rows, width), F32),
            pltpu.VMEM((READ_PAD, width), F32),
            pltpu.VMEM((READ_PAD, grid_rows), F32),
            pltpu.VMEM((READ_PAD, grid_rows), F32),
            pltpu.VMEM((8, 128), F32),
            pltpu.VMEM((VAR_PAD, grid_rows), F32),
            pltpu.VMEM((VAR_PAD, grid_rows), F32),
            pltpu.VMEM((8, 128), F32),
            pltpu.VMEM((count, 8, 128), F32),
            pltpu.VMEM((2, grid_rows, half), BF16),
            pltpu.VMEM((grid_rows, half), BF16),
            pltpu.VMEM((2, slot_rows, width), BF16),
            pltpu.VMEM((3, slot_rows, width), BF16),
            pltpu.VMEM((depth, share_rows, half), BF16),
            pltpu.VMEM((depth, share_rows, half), BF16),
            pltpu.VMEM((depth, share_rows, half), BF16),
            pltpu.VMEM((depth, share_rows, half), BF16),
            pltpu.VMEM((share_rows, half), BF16),
            pltpu.VMEM((share_rows, half), BF16),
            dma((6,)),
            dma((2, PIECES)),
            dma((2, PIECES)),
            dma((4,)),
            dma((8,)),
            dma((count,)),
            dma((count,)),
            dma((4,)),
            dma((depth,)),
            dma((depth,)),
            dma((depth,)),
            dma((depth,)),
        ],
        compiler_params=pltpu.CompilerParams(
            collective_id=0, has_side_effects=True, vmem_limit_bytes=50 * 1024 * 1024
        ),
    )(
        latent,
        project_in,
        project_out,
        decoder_weight,
        readout_weight,
        variable_weight.reshape(1, -1),
        area_weight.reshape(1, -1),
        current_state,
        target,
        block_table,
        edge_source,
        edge_weight,
    )


def solution(mesh):
    in_specs = (
        P("member", ("groups", "mp"), None),
        P(),
        P(),
        P(),
        P(),
        P(),
        P(("groups", "mp")),
        P(None, ("groups", "mp")),
        P(None, ("groups", "mp")),
        P("groups", None, None),
        P(None, ("groups", "mp")),
        P(None, ("groups", "mp")),
    )
    out_specs = (P("groups"), P("member", ("groups", "mp"), None), P(("groups", "mp"), None))
    return jax.shard_map(body, mesh=mesh, in_specs=in_specs, out_specs=out_specs, check_vma=False)
```

```python
import functools

import jax
import jax.numpy as jnp
from jax import lax
from jax.experimental import pallas as pl
from jax.experimental.pallas import tpu as pltpu
from jax.sharding import PartitionSpec as P

HEADS = 16
BLOCK_ROWS = 16
SLOTS = 2
LAT_DEV = 128
PIECES = 8
VAR_PAD = 104
READ_PAD = 128

EPSILON = 1e-05
SMOOTH = 0.01
SMOOTH_ROOT = 0.1
MASKED = -1e30
GELU_SCALE = 0.7978845608028654
GELU_CUBE = 0.044715

MESH = pl.DeviceIdType.MESH
F32 = jnp.float32
BF16 = jnp.bfloat16


def dot(a, b, dims=((1,), (0,))):
    return lax.dot_general(a, b, (dims, ((), ())), preferred_element_type=F32)


def layer_norm(values):
    row_mean = jnp.mean(values, axis=-1, keepdims=True)
    centred = values - row_mean
    inverse = lax.rsqrt(jnp.mean(centred * centred, axis=-1, keepdims=True) + EPSILON)
    return (centred * inverse, inverse)


def kernel(
    count,
    grid_total,
    tokens_hbm,
    in_hbm,
    out_hbm,
    decoder_hbm,
    readout_hbm,
    variable_hbm,
    area_hbm,
    state_hbm,
    target_hbm,
    table_hbm,
    source_hbm,
    weight_hbm,
    loss_ref,
    latent_grad_ref,
    decoder_grad_ref,
    readout_ref,
    variable_ref,
    area_ref,
    state_ref,
    target_ref,
    table_ref,
    source_ref,
    weight_ref,
    tok,
    w_in,
    w_out,
    w_dec,
    q_s,
    k_s,
    v_s,
    ctx_s,
    near_max,
    near_sum,
    near_ctx,
    chosen,
    feats,
    unit_s,
    units,
    pre_s,
    slope_s,
    readout_pad,
    state_pad,
    target_pad,
    variable_pad,
    pred_own,
    pred_other,
    loss_own,
    loss_all,
    gpre_s,
    gpre_other,
    grad_send,
    grad_recv,
    y_send,
    y_recv,
    z_send,
    z_recv,
    share_sum,
    share_own,
    share_other,
    local_sem,
    small_sem,
    halo_sem,
    pass_sem,
    feat_sem,
    pair_sem,
    loss_send_sem,
    loss_recv_sem,
    grad_sem,
    ys_sem,
    yr_sem,
    zs_sem,
    zr_sem,
):
    group = lax.axis_index("groups")
    idx = lax.axis_index("mp")
    member = lax.axis_index("member")
    other = 1 - member
    depth = count // 2
    parity = lax.rem(idx, 2)
    level = lax.div(idx, 2)
    partner = idx + 1 - 2 * parity
    width = tok.shape[2]
    half = width // 2
    share_rows = width // count
    piece = LAT_DEV // PIECES
    arrive = 2 - 2 * parity
    far = 2 - arrive
    onward = idx + 2 - 4 * parity
    origin = idx - 2 + 4 * parity
    has_onward = (onward >= 0) & (onward < count)
    has_origin = (origin >= 0) & (origin < count)
    has_low = idx > 0
    has_high = idx < count - 1

    def at(place, who):
        return (group, place, who)

    def remote(src, dst, send, recv, place, who):
        return pltpu.make_async_remote_copy(
            src_ref=src,
            dst_ref=dst,
            send_sem=send,
            recv_sem=recv,
            device_id=at(place, who),
            device_id_type=MESH,
        )

    own_copy = pltpu.make_async_copy(tokens_hbm.at[0], tok.at[1], local_sem.at[0])
    own_copy.start()
    in_copies = []
    for part in range(3):
        columns = pl.ds(part * width, width)
        in_copies.append(
            pltpu.make_async_copy(
                in_hbm.at[:, columns], w_in.at[:, columns], local_sem.at[1 + part]
            )
        )
        in_copies[-1].start()
    out_copy = pltpu.make_async_copy(out_hbm, w_out, local_sem.at[4])
    out_copy.start()
    dec_copy = pltpu.make_async_copy(decoder_hbm, w_dec, local_sem.at[5])
    dec_copy.start()

    small_copies = []
    for i, (src, dst) in enumerate(
        (
            (table_hbm, table_ref),
            (source_hbm, source_ref),
            (weight_hbm, weight_ref),
            (readout_hbm, readout_ref),
            (state_hbm, state_ref),
            (target_hbm, target_ref),
            (variable_hbm, variable_ref),
            (area_hbm, area_ref),
        )
    ):
        small_copies.append(pltpu.make_async_copy(src, dst, small_sem.at[i]))
        small_copies[-1].start()

    barrier = pltpu.get_barrier_semaphore()
    for step in range(1, count):
        pl.semaphore_signal(
            barrier,
            inc=1,
            device_id=at(lax.rem(idx + step, count), member),
            device_id_type=MESH,
        )
    pl.semaphore_signal(barrier, inc=1, device_id=at(idx, other), device_id_type=MESH)
    pl.semaphore_wait(barrier, count)

    def halo_copy(c):
        rows = pl.ds(c * piece, piece)
        return remote(
            tokens_hbm.at[0, rows],
            tok.at[far, rows],
            halo_sem.at[0, c],
            halo_sem.at[1, c],
            partner,
            member,
        )

    def pass_copy(c):
        rows = pl.ds(c * piece, piece)
        return remote(
            tok.at[arrive, rows],
            tok.at[far, rows],
            pass_sem.at[0, c],
            pass_sem.at[1, c],
            onward,
            member,
        )

    for c in range(PIECES):
        halo_copy(c).start()

    @pl.when(jnp.logical_not(has_origin))
    def _():
        tok[far] = jnp.zeros((LAT_DEV, width), BF16)

    @pl.when(jnp.logical_not(has_low))
    def _():
        feats[0] = jnp.zeros(feats.shape[1:], BF16)
        grad_recv[0] = jnp.zeros(grad_recv.shape[1:], BF16)

    @pl.when(jnp.logical_not(has_high))
    def _():
        feats[2] = jnp.zeros(feats.shape[1:], BF16)
        grad_recv[2] = jnp.zeros(grad_recv.shape[1:], BF16)

    def relay(c):
        halo_copy(c).wait_recv()

        @pl.when(has_onward)
        def _():
            pass_copy(c).start()

    own_copy.wait()
    normed = layer_norm(tok[1].astype(F32))[0].astype(BF16)
    in_copies[0].wait()
    q_s[...] = (dot(normed, w_in[:, :width]) * (HEADS / width) ** 0.5).astype(BF16)
    relay(0)
    relay(1)
    in_copies[1].wait()
    k_s[0:LAT_DEV] = dot(normed, w_in[:, width : 2 * width]).astype(BF16)
    relay(2)
    relay(3)
    in_copies[2].wait()
    v_s[0:LAT_DEV] = dot(normed, w_in[:, 2 * width :]).astype(BF16)

    readout_pad[...] = jnp.zeros(readout_pad.shape, F32)
    state_pad[...] = jnp.zeros(state_pad.shape, F32)
    target_pad[...] = jnp.zeros(target_pad.shape, F32)
    variable_pad[...] = jnp.zeros(variable_pad.shape, F32)
    for copy in small_copies:
        copy.wait()
    variables = readout_ref.shape[0]
    readout_pad[0:variables] = readout_ref[...].astype(F32)
    state_pad[0:variables] = state_ref[...]
    target_pad[0:variables] = target_ref[...]
    variable_pad[0:1, 0:variables] = variable_ref[...]
    for c in range(4, PIECES):
        relay(c)

    def keys_values(slot, rows):
        halo = layer_norm(tok[slot].astype(F32))[0].astype(BF16)
        k_s[rows] = dot(halo, w_in[:, width : 2 * width]).astype(BF16)
        v_s[rows] = dot(halo, w_in[:, 2 * width :]).astype(BF16)

    keys_values(arrive, slice(LAT_DEV, 2 * LAT_DEV))

    query_at = lax.broadcasted_iota(jnp.int32, (LAT_DEV, LAT_DEV), 0)
    key_at = lax.broadcasted_iota(jnp.int32, (LAT_DEV, LAT_DEV), 1)

    def bias_of(slot):
        apart = key_at + (slot - 1) * LAT_DEV - query_at
        place = key_at + (idx + slot - 1) * LAT_DEV
        allowed = (
            (apart >= -LAT_DEV) & (apart <= LAT_DEV) & (place >= 0) & (place < count * LAT_DEV)
        )
        bias = jnp.where(allowed, 0.0, MASKED)
        return jnp.concatenate([bias, bias], axis=0)

    first_head = lax.broadcasted_iota(jnp.int32, (LAT_DEV, 128), 1) < 64
    near_bias = jnp.concatenate([jnp.zeros((2 * LAT_DEV, LAT_DEV), F32), bias_of(arrive)], axis=1)

    def pair_queries(columns):
        queries = q_s[:, columns].astype(F32)
        return jnp.concatenate(
            [jnp.where(first_head, queries, 0.0), jnp.where(first_head, 0.0, queries)], axis=0
        ).astype(BF16)

    for pair in range(width // 128):
        columns = slice(pair * 128, (pair + 1) * 128)
        scores = (
            dot(pair_queries(columns), k_s[: 2 * LAT_DEV, columns], ((1,), (1,))) + near_bias
        )
        largest = jnp.max(scores, axis=-1, keepdims=True)
        powers = jnp.exp(scores - largest)
        total = jnp.sum(powers, axis=-1, keepdims=True)
        near_max[pair] = jnp.broadcast_to(largest, (2 * LAT_DEV, 128))
        near_sum[pair] = jnp.broadcast_to(total, (2 * LAT_DEV, 128))
        near_ctx[pair] = dot(powers.astype(BF16), v_s[: 2 * LAT_DEV, columns])

    @pl.when(has_origin)
    def _():
        for c in range(PIECES):
            pass_copy(c).wait_recv()

    keys_values(far, slice(2 * LAT_DEV, 3 * LAT_DEV))
    far_bias = bias_of(far)
    for pair in range(width // 128):
        columns = slice(pair * 128, (pair + 1) * 128)
        scores = dot(pair_queries(columns), k_s[2 * LAT_DEV :, columns], ((1,), (1,))) + far_bias
        largest = jnp.maximum(near_max[pair], jnp.max(scores, axis=-1, keepdims=True))
        powers = jnp.exp(scores - largest)
        shrink = jnp.exp(near_max[pair] - largest)
        total = near_sum[pair] * shrink + jnp.sum(powers, axis=-1, keepdims=True)
        context = near_ctx[pair] * shrink + dot(powers.astype(BF16), v_s[2 * LAT_DEV :, columns])
        context = context / total
        ctx_s[:, columns] = jnp.where(
            first_head, context[:LAT_DEV], context[LAT_DEV:]
        ).astype(BF16)

    out_copy.wait()
    mixed = dot(ctx_s[...], w_out[...])
    latent_out = (tok[1].astype(F32) + mixed).astype(BF16)

    below = jnp.maximum(idx - 1, 0)
    above = jnp.minimum(idx + 1, count - 1)
    row_at = lax.broadcasted_iota(jnp.int32, (BLOCK_ROWS, LAT_DEV), 0)
    column_at = lax.broadcasted_iota(jnp.int32, (BLOCK_ROWS, LAT_DEV), 1)
    picks = []
    for tile, j, live in ((below, 2, has_low), (idx, 1, True), (above, 0, has_high)):
        for c in range(SLOTS):
            hit = column_at == row_at + table_ref[j, c, tile] * BLOCK_ROWS
            pick = jnp.where(hit, 1.0, 0.0)
            if live is not True:
                pick = pick * jnp.where(live, 1.0, 0.0)
            picks.append(pick)
    pick = jnp.concatenate(picks, axis=0).astype(BF16)
    slot_rows = SLOTS * BLOCK_ROWS
    chosen_rows = dot(pick, latent_out).astype(BF16)
    for j in range(3):
        chosen[j] = chosen_rows[j * slot_rows : (j + 1) * slot_rows]
    feats[1] = chosen_rows[slot_rows : 2 * slot_rows]

    feat_down = remote(
        chosen.at[0], feats.at[2], feat_sem.at[0], feat_sem.at[1], idx - 1, member
    )
    feat_up = remote(chosen.at[2], feats.at[0], feat_sem.at[2], feat_sem.at[3], idx + 1, member)

    @pl.when(has_low)
    def _():
        feat_down.start()

    @pl.when(has_high)
    def _():
        feat_up.start()

    grid_rows = source_ref.shape[1]
    position = lax.broadcasted_iota(jnp.int32, (3 * slot_rows, grid_rows), 0)
    spread = jnp.zeros((3 * slot_rows, grid_rows), F32)
    for k in range(3):
        spread = spread + jnp.where(
            position == source_ref[k : k + 1, :], weight_ref[k : k + 1, :], 0.0
        )
    spread_high = spread.astype(BF16)
    spread_low = (spread - spread_high.astype(F32)).astype(BF16)
    readout = readout_pad[...].astype(BF16)
    diagonal = lax.broadcasted_iota(jnp.int32, (READ_PAD, 128), 0) == lax.broadcasted_iota(
        jnp.int32, (READ_PAD, 128), 1
    )
    variable = jnp.sum(jnp.where(diagonal, variable_pad[0:1, :], 0.0), axis=1, keepdims=True)
    loss_weights = variable * area_ref[...]

    @pl.when(has_high)
    def _():
        feat_down_in = remote(
            chosen.at[0], feats.at[2], feat_sem.at[0], feat_sem.at[1], idx + 1, member
        )
        feat_down_in.wait_recv()

    @pl.when(has_low)
    def _():
        feat_up_in = remote(
            chosen.at[2], feats.at[0], feat_sem.at[2], feat_sem.at[3], idx - 1, member
        )
        feat_up_in.wait_recv()

    all_rows = feats[...].reshape(3 * slot_rows, width)
    aggregate = dot(
        jnp.concatenate([spread_high, spread_low], axis=0),
        jnp.concatenate([all_rows, all_rows], axis=0),
        ((0,), (0,)),
    )
    unit, inverse = layer_norm(aggregate)
    unit_s[...] = unit
    dec_copy.wait()
    pre = dot(unit.astype(BF16), w_dec[...])
    pre_s[...] = pre
    hidden = (
        0.5 * pre * (1.0 + jnp.tanh(GELU_SCALE * (pre + GELU_CUBE * pre * pre * pre)))
    ).astype(BF16)
    prediction = state_pad[...] + dot(readout, hidden, ((1,), (1,)))
    pred_own[...] = prediction[:VAR_PAD]
    pred_copy = remote(pred_own, pred_other, pair_sem.at[2], pair_sem.at[3], idx, other)
    pred_copy.start()

    units[0] = jnp.transpose(unit_s[...]).astype(BF16)
    unit_copy = remote(units.at[0], units.at[1], pair_sem.at[0], pair_sem.at[1], idx, other)
    unit_copy.start()

    pre = pre_s[...]
    square = pre * pre
    bend = jnp.tanh(GELU_SCALE * (pre + GELU_CUBE * pre * square))
    slope_s[...] = 0.5 * (1.0 + bend) + 0.5 * pre * (1.0 - bend * bend) * (
        GELU_SCALE * (1.0 + 3.0 * GELU_CUBE * square)
    )

    pred_copy.wait_recv()
    mine = pred_own[...]
    theirs = pred_other[...]
    target = target_pad[...][:VAR_PAD]
    weights = loss_weights[:VAR_PAD]
    miss = mine - target
    miss_other = theirs - target
    apart = mine - theirs
    miss_root = jnp.sqrt(miss * miss + SMOOTH)
    other_root = jnp.sqrt(miss_other * miss_other + SMOOTH)
    apart_root = jnp.sqrt(apart * apart + SMOOTH)
    objective = weights * (
        ((miss_root - SMOOTH_ROOT) + (other_root - SMOOTH_ROOT)) * 0.5
        - (apart_root - SMOOTH_ROOT) * 0.5
    )
    terms = jnp.sum(objective.reshape(VAR_PAD // 8, 8, grid_rows), axis=0)
    folded = terms[:, :128]
    for start in range(128, grid_rows, 128):
        folded = folded + terms[:, start : start + 128]
    loss_own[...] = folded
    loss_all[idx] = folded
    grad_prediction = weights * (miss / miss_root * 0.5 - apart / apart_root * 0.5)
    grad_prediction = jnp.concatenate(
        [grad_prediction, jnp.zeros((READ_PAD - VAR_PAD, grid_rows), F32)], axis=0
    ).astype(BF16)

    grad_hidden = dot(grad_prediction, readout, ((0,), (0,)))
    grad_pre = (grad_hidden * slope_s[...]).astype(BF16)
    gpre_s[0] = grad_pre[:, :half]
    gpre_s[1] = grad_pre[:, half:]
    gpre_copy = remote(
        gpre_s.at[other], gpre_other, pair_sem.at[4], pair_sem.at[5], idx, other
    )
    gpre_copy.start()

    def loss_copy(step):
        goal = lax.rem(idx + step, count)
        return remote(
            loss_own,
            loss_all.at[idx],
            loss_send_sem.at[step],
            loss_recv_sem.at[step],
            goal,
            member,
        )

    def loss_in(step):
        start = lax.rem(idx + count - step, count)
        return remote(
            loss_own,
            loss_all.at[start],
            loss_send_sem.at[step],
            loss_recv_sem.at[step],
            start,
            member,
        )

    for step in range(1, count):
        loss_copy(step).start()

    pre_s[...] = dot(grad_pre, w_dec[...], ((1,), (1,)))

    unit_copy.wait_recv()
    gpre_copy.wait_recv()
    grad_here = jnp.concatenate([gpre_s[member], gpre_other[...]], axis=0)

    def weight_rows(chunk):
        rows = pl.ds(pl.multiple_of(chunk * share_rows, share_rows), share_rows)
        return dot(jnp.concatenate([units[0, rows], units[1, rows]], axis=1), grad_here)

    def y_copy(step):
        return remote(
            y_send.at[step], y_recv.at[step], ys_sem.at[step], yr_sem.at[step], partner, member
        )

    rising = depth - 1 - level
    falls_first = level >= depth // 2

    def target_at(step):
        fall = jnp.where(step < level, step, depth - 1 - (step - level))
        rise = jnp.where(step < rising, depth - 1 - step, step - rising)
        return jnp.where(step == depth - 1, level, jnp.where(falls_first, fall, rise))

    def z_copy(step):
        goal = target_at(step)
        up = goal > level
        hop = jnp.where(up, level + 1, level - 1)
        slot = jnp.where(jnp.logical_not(up) & (hop == goal), depth, goal)
        return remote(
            z_send.at[step],
            z_recv.at[slot],
            zs_sem.at[step],
            zr_sem.at[slot],
            2 * hop + parity,
            member,
        )

    def z_wait(slot):
        remote(
            z_send.at[0], z_recv.at[slot], zs_sem.at[0], zr_sem.at[slot], partner, member
        ).wait_recv()

    def send_partner(step, carry):
        chunk = 2 * target_at(step) + (1 - parity)
        y_send[step] = weight_rows(chunk).astype(BF16)
        y_copy(step).start()
        return carry

    lax.fori_loop(0, depth, send_partner, 0)

    grad_unit = pre_s[...]
    unit = unit_s[...]
    grad_aggregate = inverse * (
        grad_unit
        - jnp.mean(grad_unit, axis=-1, keepdims=True)
        - unit * jnp.mean(grad_unit * unit, axis=-1, keepdims=True)
    )
    rounded = grad_aggregate.astype(BF16)
    tile_grad = (dot(spread_high, rounded) + dot(spread_low, rounded)).astype(BF16)
    grad_send[0] = tile_grad[:slot_rows]
    grad_send[1] = tile_grad[2 * slot_rows :]
    grad_recv[1] = tile_grad[slot_rows : 2 * slot_rows]
    grad_down = remote(
        grad_send.at[0], grad_recv.at[2], grad_sem.at[0], grad_sem.at[1], idx - 1, member
    )
    grad_up = remote(
        grad_send.at[1], grad_recv.at[0], grad_sem.at[2], grad_sem.at[3], idx + 1, member
    )

    @pl.when(has_low)
    def _():
        grad_down.start()

    @pl.when(has_high)
    def _():
        grad_up.start()

    def send_level(step, carry):
        goal = target_at(step)
        share_sum[...] = weight_rows(2 * goal + parity)
        y_copy(step).wait_recv()
        share_sum[...] += y_recv[step].astype(F32)

        @pl.when(((goal > level) & (level > 0)) | ((goal < level) & (level < depth - 1)))
        def _():
            z_wait(goal)
            share_sum[...] += z_recv[goal].astype(F32)

        z_send[step] = share_sum[...].astype(BF16)
        z_copy(step).start()
        return carry

    lax.fori_loop(0, depth - 1, send_level, 0)
    share_sum[...] = weight_rows(idx)
    y_copy(depth - 1).wait_recv()
    share_sum[...] += y_recv[depth - 1].astype(F32)

    @pl.when(has_high)
    def _():
        remote(
            grad_send.at[0], grad_recv.at[2], grad_sem.at[0], grad_sem.at[1], idx + 1, member
        ).wait_recv()

    @pl.when(has_low)
    def _():
        remote(
            grad_send.at[1], grad_recv.at[0], grad_sem.at[2], grad_sem.at[3], idx - 1, member
        ).wait_recv()

    latent_grad_ref[0] = dot(
        pick, grad_recv[...].reshape(3 * slot_rows, width), ((0,), (0,))
    )

    for step in range(1, count):
        loss_in(step).wait_recv()
    loss_sum = loss_all[0]
    for step in range(1, count):
        loss_sum = loss_sum + loss_all[step]
    loss_ref[0] = jnp.sum(loss_sum) / grid_total

    @pl.when(level > 0)
    def _():
        z_wait(level)
        share_sum[...] += z_recv[level].astype(F32)

    @pl.when(level < depth - 1)
    def _():
        z_wait(depth)
        share_sum[...] += z_recv[depth].astype(F32)

    share_own[...] = share_sum[...].astype(BF16)
    share_copy = remote(share_own, share_other, pair_sem.at[6], pair_sem.at[7], idx, other)
    share_copy.start()
    own_columns = pl.ds(pl.multiple_of(member * half, half), half)
    other_columns = pl.ds(pl.multiple_of(other * half, half), half)
    decoder_grad_ref[:, own_columns] = share_own[...].astype(F32)
    share_copy.wait_recv()
    decoder_grad_ref[:, other_columns] = share_other[...].astype(F32)

    for c in range(PIECES):
        halo_copy(c).wait_send()

    @pl.when(has_onward)
    def _():
        for c in range(PIECES):
            pass_copy(c).wait_send()

    @pl.when(has_low)
    def _():
        feat_down.wait_send()
        grad_down.wait_send()

    @pl.when(has_high)
    def _():
        feat_up.wait_send()
        grad_up.wait_send()

    unit_copy.wait_send()
    pred_copy.wait_send()
    gpre_copy.wait_send()
    share_copy.wait_send()
    for step in range(1, count):
        loss_copy(step).wait_send()
    for step in range(depth):
        y_copy(step).wait_send()
    for step in range(depth - 1):
        z_copy(step).wait_send()


def body(
    latent,
    project_in,
    project_out,
    decoder_weight,
    readout_weight,
    variable_weight,
    area_weight,
    current_state,
    target,
    block_table,
    edge_source,
    edge_weight,
):
    count = lax.axis_size("mp")
    width = latent.shape[2]
    half = width // 2
    depth = count // 2
    share_rows = width // count
    grid_rows = edge_source.shape[1]
    slot_rows = SLOTS * BLOCK_ROWS
    hbm = pl.BlockSpec(memory_space=pltpu.MemorySpace.HBM)
    vmem = pl.BlockSpec(memory_space=pltpu.VMEM)
    smem = pl.BlockSpec(memory_space=pltpu.SMEM)
    dma = pltpu.SemaphoreType.DMA
    return pl.pallas_call(
        functools.partial(kernel, count, float(count * grid_rows)),
        out_shape=(
            jax.ShapeDtypeStruct((1,), F32),
            jax.ShapeDtypeStruct((1, LAT_DEV, width), F32),
            jax.ShapeDtypeStruct((share_rows, width), F32),
        ),
        in_specs=[hbm] * 12,
        out_specs=(smem, vmem, vmem),
        scratch_shapes=[
            pltpu.VMEM(readout_weight.shape, BF16),
            pltpu.VMEM((1, variable_weight.shape[0]), F32),
            pltpu.VMEM((1, grid_rows), F32),
            pltpu.VMEM(current_state.shape, F32),
            pltpu.VMEM(target.shape, F32),
            pltpu.SMEM((3, SLOTS, count), jnp.int32),
            pltpu.VMEM(edge_source.shape, jnp.int32),
            pltpu.VMEM(edge_weight.shape, F32),
            pltpu.VMEM((3, LAT_DEV, width), BF16),
            pltpu.VMEM((width, 3 * width), BF16),
            pltpu.VMEM((width, width), BF16),
            pltpu.VMEM((width, width), BF16),
            pltpu.VMEM((LAT_DEV, width), BF16),
            pltpu.VMEM((3 * LAT_DEV, width), BF16),
            pltpu.VMEM((3 * LAT_DEV, width), BF16),
            pltpu.VMEM((LAT_DEV, width), BF16),
            pltpu.VMEM((width // 128, 2 * LAT_DEV, 128), F32),
            pltpu.VMEM((width // 128, 2 * LAT_DEV, 128), F32),
            pltpu.VMEM((width // 128, 2 * LAT_DEV, 128), F32),
            pltpu.VMEM((3, slot_rows, width), BF16),
            pltpu.VMEM((3, slot_rows, width), BF16),
            pltpu.VMEM((grid_rows, width), F32),
            pltpu.VMEM((2, width, grid_rows), BF16),
            pltpu.VMEM((grid_rows, width), F32),
            pltpu.VMEM((grid_rows, width), F32),
            pltpu.VMEM((READ_PAD, width), F32),
            pltpu.VMEM((READ_PAD, grid_rows), F32),
            pltpu.VMEM((READ_PAD, grid_rows), F32),
            pltpu.VMEM((8, 128), F32),
            pltpu.VMEM((VAR_PAD, grid_rows), F32),
            pltpu.VMEM((VAR_PAD, grid_rows), F32),
            pltpu.VMEM((8, 128), F32),
            pltpu.VMEM((count, 8, 128), F32),
            pltpu.VMEM((2, grid_rows, half), BF16),
            pltpu.VMEM((grid_rows, half), BF16),
            pltpu.VMEM((2, slot_rows, width), BF16),
            pltpu.VMEM((3, slot_rows, width), BF16),
            pltpu.VMEM((depth, share_rows, half), BF16),
            pltpu.VMEM((depth, share_rows, half), BF16),
            pltpu.VMEM((depth, share_rows, half), BF16),
            pltpu.VMEM((depth + 1, share_rows, half), BF16),
            pltpu.VMEM((share_rows, half), F32),
            pltpu.VMEM((share_rows, half), BF16),
            pltpu.VMEM((share_rows, half), BF16),
            dma((6,)),
            dma((8,)),
            dma((2, PIECES)),
            dma((2, PIECES)),
            dma((4,)),
            dma((8,)),
            dma((count,)),
            dma((count,)),
            dma((4,)),
            dma((depth,)),
            dma((depth,)),
            dma((depth,)),
            dma((depth + 1,)),
        ],
        compiler_params=pltpu.CompilerParams(
            collective_id=0, has_side_effects=True, vmem_limit_bytes=62 * 1024 * 1024
        ),
    )(
        latent,
        project_in,
        project_out,
        decoder_weight,
        readout_weight,
        variable_weight.reshape(1, -1),
        area_weight.reshape(1, -1),
        current_state,
        target,
        jnp.transpose(block_table, (1, 2, 0)),
        edge_source,
        edge_weight,
    )


def solution(mesh):
    in_specs = (
        P("member", ("groups", "mp"), None),
        P(),
        P(),
        P(),
        P(),
        P(),
        P(("groups", "mp")),
        P(None, ("groups", "mp")),
        P(None, ("groups", "mp")),
        P("groups", None, None),
        P(None, ("groups", "mp")),
        P(None, ("groups", "mp")),
    )
    out_specs = (P("groups"), P("member", ("groups", "mp"), None), P(("groups", "mp"), None))
    return jax.shard_map(body, mesh=mesh, in_specs=in_specs, out_specs=out_specs, check_vma=False)
```

```python
import functools

import jax
import jax.numpy as jnp
from jax import lax
from jax.experimental import pallas as pl
from jax.experimental.pallas import tpu as pltpu
from jax.sharding import PartitionSpec as P

HEADS = 16
BLOCK_ROWS = 16
SLOTS = 2
LAT_DEV = 128
PIECES = 8
VAR_PAD = 104
READ_PAD = 128

EPSILON = 1e-05
SMOOTH = 0.01
SMOOTH_ROOT = 0.1
MASKED = -1e30
GELU_SCALE = 0.7978845608028654
GELU_CUBE = 0.044715

MESH = pl.DeviceIdType.MESH
F32 = jnp.float32
BF16 = jnp.bfloat16


def dot(a, b, dims=((1,), (0,))):
    return lax.dot_general(a, b, (dims, ((), ())), preferred_element_type=F32)


def layer_norm(values):
    row_mean = jnp.mean(values, axis=-1, keepdims=True)
    centred = values - row_mean
    inverse = lax.rsqrt(jnp.mean(centred * centred, axis=-1, keepdims=True) + EPSILON)
    return (centred * inverse, inverse)


def kernel(
    count,
    grid_total,
    tokens_hbm,
    in_hbm,
    out_hbm,
    decoder_hbm,
    readout_hbm,
    variable_hbm,
    area_hbm,
    state_hbm,
    target_hbm,
    table_hbm,
    source_hbm,
    weight_hbm,
    loss_ref,
    rows_ref,
    pick_ref,
    share_ref,
    readout_ref,
    variable_ref,
    area_ref,
    state_ref,
    target_ref,
    table_ref,
    source_ref,
    weight_ref,
    tok,
    w_in,
    w_out,
    w_dec,
    q_s,
    k_s,
    v_s,
    ctx_s,
    near_max,
    near_sum,
    near_ctx,
    chosen,
    feats,
    unit_s,
    units,
    pre_s,
    slope_s,
    readout_pad,
    state_pad,
    target_pad,
    variable_pad,
    pred_own,
    pred_other,
    loss_own,
    loss_all,
    gpre_s,
    gpre_other,
    grad_send,
    grad_recv,
    y_send,
    y_recv,
    z_send,
    z_recv,
    share_sum,
    share_own,
    share_other,
    local_sem,
    small_sem,
    halo_sem,
    pass_sem,
    feat_sem,
    pair_sem,
    loss_send_sem,
    loss_recv_sem,
    grad_sem,
    ys_sem,
    yr_sem,
    zs_sem,
    zr_sem,
):
    group = lax.axis_index("groups")
    idx = lax.axis_index("mp")
    member = lax.axis_index("member")
    other = 1 - member
    depth = count // 2
    parity = lax.rem(idx, 2)
    level = lax.div(idx, 2)
    partner = idx + 1 - 2 * parity
    width = tok.shape[2]
    half = width // 2
    share_rows = width // count
    piece = LAT_DEV // PIECES
    arrive = 2 - 2 * parity
    far = 2 - arrive
    onward = idx + 2 - 4 * parity
    origin = idx - 2 + 4 * parity
    has_onward = (onward >= 0) & (onward < count)
    has_origin = (origin >= 0) & (origin < count)
    has_low = idx > 0
    has_high = idx < count - 1

    def at(place, who):
        return (group, place, who)

    def remote(src, dst, send, recv, place, who):
        return pltpu.make_async_remote_copy(
            src_ref=src,
            dst_ref=dst,
            send_sem=send,
            recv_sem=recv,
            device_id=at(place, who),
            device_id_type=MESH,
        )

    own_copy = pltpu.make_async_copy(tokens_hbm.at[0], tok.at[1], local_sem.at[0])
    own_copy.start()
    in_copies = []
    for part in range(3):
        columns = pl.ds(part * width, width)
        in_copies.append(
            pltpu.make_async_copy(
                in_hbm.at[:, columns], w_in.at[:, columns], local_sem.at[1 + part]
            )
        )
        in_copies[-1].start()
    out_copy = pltpu.make_async_copy(out_hbm, w_out, local_sem.at[4])
    out_copy.start()
    dec_copy = pltpu.make_async_copy(decoder_hbm, w_dec, local_sem.at[5])
    dec_copy.start()

    small_copies = []
    for i, (src, dst) in enumerate(
        (
            (table_hbm, table_ref),
            (source_hbm, source_ref),
            (weight_hbm, weight_ref),
            (readout_hbm, readout_ref),
            (state_hbm, state_ref),
            (target_hbm, target_ref),
            (variable_hbm, variable_ref),
            (area_hbm, area_ref),
        )
    ):
        small_copies.append(pltpu.make_async_copy(src, dst, small_sem.at[i]))
        small_copies[-1].start()

    barrier = pltpu.get_barrier_semaphore()
    for step in range(1, count):
        pl.semaphore_signal(
            barrier,
            inc=1,
            device_id=at(lax.rem(idx + step, count), member),
            device_id_type=MESH,
        )
    pl.semaphore_signal(barrier, inc=1, device_id=at(idx, other), device_id_type=MESH)
    pl.semaphore_wait(barrier, count)

    def halo_copy(c):
        rows = pl.ds(c * piece, piece)
        return remote(
            tokens_hbm.at[0, rows],
            tok.at[far, rows],
            halo_sem.at[0, c],
            halo_sem.at[1, c],
            partner,
            member,
        )

    def pass_copy(c):
        rows = pl.ds(c * piece, piece)
        return remote(
            tok.at[arrive, rows],
            tok.at[far, rows],
            pass_sem.at[0, c],
            pass_sem.at[1, c],
            onward,
            member,
        )

    for c in range(PIECES):
        halo_copy(c).start()

    @pl.when(jnp.logical_not(has_origin))
    def _():
        tok[far] = jnp.zeros((LAT_DEV, width), BF16)

    @pl.when(jnp.logical_not(has_low))
    def _():
        feats[0] = jnp.zeros(feats.shape[1:], BF16)
        grad_recv[0] = jnp.zeros(grad_recv.shape[1:], BF16)

    @pl.when(jnp.logical_not(has_high))
    def _():
        feats[2] = jnp.zeros(feats.shape[1:], BF16)
        grad_recv[2] = jnp.zeros(grad_recv.shape[1:], BF16)

    def relay(c):
        halo_copy(c).wait_recv()

        @pl.when(has_onward)
        def _():
            pass_copy(c).start()

    own_copy.wait()
    normed = layer_norm(tok[1].astype(F32))[0].astype(BF16)
    in_copies[0].wait()
    q_s[...] = (dot(normed, w_in[:, :width]) * (HEADS / width) ** 0.5).astype(BF16)
    relay(0)
    relay(1)
    in_copies[1].wait()
    k_s[0:LAT_DEV] = dot(normed, w_in[:, width : 2 * width]).astype(BF16)
    relay(2)
    relay(3)
    in_copies[2].wait()
    v_s[0:LAT_DEV] = dot(normed, w_in[:, 2 * width :]).astype(BF16)

    readout_pad[...] = jnp.zeros(readout_pad.shape, F32)
    state_pad[...] = jnp.zeros(state_pad.shape, F32)
    target_pad[...] = jnp.zeros(target_pad.shape, F32)
    variable_pad[...] = jnp.zeros(variable_pad.shape, F32)
    for copy in small_copies:
        copy.wait()
    variables = readout_ref.shape[0]
    readout_pad[0:variables] = readout_ref[...].astype(F32)
    state_pad[0:variables] = state_ref[...]
    target_pad[0:variables] = target_ref[...]
    variable_pad[0:1, 0:variables] = variable_ref[...]
    for c in range(4, PIECES):
        relay(c)

    def keys_values(slot, rows):
        halo = layer_norm(tok[slot].astype(F32))[0].astype(BF16)
        k_s[rows] = dot(halo, w_in[:, width : 2 * width]).astype(BF16)
        v_s[rows] = dot(halo, w_in[:, 2 * width :]).astype(BF16)

    keys_values(arrive, slice(LAT_DEV, 2 * LAT_DEV))

    query_at = lax.broadcasted_iota(jnp.int32, (LAT_DEV, LAT_DEV), 0)
    key_at = lax.broadcasted_iota(jnp.int32, (LAT_DEV, LAT_DEV), 1)

    def bias_of(slot):
        apart = key_at + (slot - 1) * LAT_DEV - query_at
        place = key_at + (idx + slot - 1) * LAT_DEV
        allowed = (
            (apart >= -LAT_DEV) & (apart <= LAT_DEV) & (place >= 0) & (place < count * LAT_DEV)
        )
        bias = jnp.where(allowed, 0.0, MASKED)
        return jnp.concatenate([bias, bias], axis=0)

    first_head = lax.broadcasted_iota(jnp.int32, (LAT_DEV, 128), 1) < 64
    near_bias = jnp.concatenate([jnp.zeros((2 * LAT_DEV, LAT_DEV), F32), bias_of(arrive)], axis=1)

    def pair_queries(columns):
        queries = q_s[:, columns].astype(F32)
        return jnp.concatenate(
            [jnp.where(first_head, queries, 0.0), jnp.where(first_head, 0.0, queries)], axis=0
        ).astype(BF16)

    for pair in range(width // 128):
        columns = slice(pair * 128, (pair + 1) * 128)
        scores = (
            dot(pair_queries(columns), k_s[: 2 * LAT_DEV, columns], ((1,), (1,))) + near_bias
        )
        largest = jnp.max(scores, axis=-1, keepdims=True)
        powers = jnp.exp(scores - largest)
        total = jnp.sum(powers, axis=-1, keepdims=True)
        near_max[pair] = jnp.broadcast_to(largest, (2 * LAT_DEV, 128))
        near_sum[pair] = jnp.broadcast_to(total, (2 * LAT_DEV, 128))
        near_ctx[pair] = dot(powers.astype(BF16), v_s[: 2 * LAT_DEV, columns])

    below = jnp.maximum(idx - 1, 0)
    above = jnp.minimum(idx + 1, count - 1)
    row_at = lax.broadcasted_iota(jnp.int32, (BLOCK_ROWS, LAT_DEV), 0)
    column_at = lax.broadcasted_iota(jnp.int32, (BLOCK_ROWS, LAT_DEV), 1)
    picks = []
    for tile, j, live in ((below, 2, has_low), (idx, 1, True), (above, 0, has_high)):
        for c in range(SLOTS):
            hit = column_at == row_at + table_ref[j, c, tile] * BLOCK_ROWS
            pick = jnp.where(hit, 1.0, 0.0)
            if live is not True:
                pick = pick * jnp.where(live, 1.0, 0.0)
            picks.append(pick)
    pick = jnp.concatenate(picks, axis=0).astype(BF16)
    slot_rows = SLOTS * BLOCK_ROWS
    pick_ref[...] = pick

    @pl.when(has_origin)
    def _():
        for c in range(PIECES):
            pass_copy(c).wait_recv()

    keys_values(far, slice(2 * LAT_DEV, 3 * LAT_DEV))
    far_bias = bias_of(far)
    for pair in range(width // 128):
        columns = slice(pair * 128, (pair + 1) * 128)
        scores = dot(pair_queries(columns), k_s[2 * LAT_DEV :, columns], ((1,), (1,))) + far_bias
        largest = jnp.maximum(near_max[pair], jnp.max(scores, axis=-1, keepdims=True))
        powers = jnp.exp(scores - largest)
        shrink = jnp.exp(near_max[pair] - largest)
        total = near_sum[pair] * shrink + jnp.sum(powers, axis=-1, keepdims=True)
        context = near_ctx[pair] * shrink + dot(powers.astype(BF16), v_s[2 * LAT_DEV :, columns])
        context = context / total
        ctx_s[:, columns] = jnp.where(
            first_head, context[:LAT_DEV], context[LAT_DEV:]
        ).astype(BF16)

    out_copy.wait()
    context = ctx_s[...]

    def feat_copies(part):
        columns = slice(part * half, (part + 1) * half)
        down = remote(
            chosen.at[0, :, columns],
            feats.at[2, :, columns],
            feat_sem.at[0, part],
            feat_sem.at[1, part],
            idx - 1,
            member,
        )
        up = remote(
            chosen.at[2, :, columns],
            feats.at[0, :, columns],
            feat_sem.at[2, part],
            feat_sem.at[3, part],
            idx + 1,
            member,
        )
        return (down, up)

    for part in range(2):
        columns = slice(part * half, (part + 1) * half)
        mixed = dot(context, w_out[:, columns])
        latent_out = (tok[1, :, columns].astype(F32) + mixed).astype(BF16)
        chosen_rows = dot(pick, latent_out).astype(BF16)
        for j in range(3):
            chosen[j, :, columns] = chosen_rows[j * slot_rows : (j + 1) * slot_rows]
        feats[1, :, columns] = chosen_rows[slot_rows : 2 * slot_rows]

        @pl.when(has_low)
        def _():
            feat_copies(part)[0].start()

        @pl.when(has_high)
        def _():
            feat_copies(part)[1].start()

    grid_rows = source_ref.shape[1]
    position = lax.broadcasted_iota(jnp.int32, (3 * slot_rows, grid_rows), 0)
    spread = jnp.zeros((3 * slot_rows, grid_rows), F32)
    for k in range(3):
        spread = spread + jnp.where(
            position == source_ref[k : k + 1, :], weight_ref[k : k + 1, :], 0.0
        )
    spread_high = spread.astype(BF16)
    spread_low = (spread - spread_high.astype(F32)).astype(BF16)
    readout = readout_pad[...].astype(BF16)
    diagonal = lax.broadcasted_iota(jnp.int32, (READ_PAD, 128), 0) == lax.broadcasted_iota(
        jnp.int32, (READ_PAD, 128), 1
    )
    variable = jnp.sum(jnp.where(diagonal, variable_pad[0:1, :], 0.0), axis=1, keepdims=True)
    loss_weights = variable * area_ref[...]

    spread_both = jnp.concatenate([spread_high, spread_low], axis=0)
    for part in range(2):
        columns = slice(part * half, (part + 1) * half)

        @pl.when(has_high)
        def _():
            feat_copies(part)[0].wait_recv()

        @pl.when(has_low)
        def _():
            feat_copies(part)[1].wait_recv()

        all_rows = feats[:, :, columns].reshape(3 * slot_rows, half)
        unit_s[:, columns] = dot(
            spread_both, jnp.concatenate([all_rows, all_rows], axis=0), ((0,), (0,))
        )
    aggregate = unit_s[...]
    unit, inverse = layer_norm(aggregate)
    unit_s[...] = unit
    dec_copy.wait()
    pre = dot(unit.astype(BF16), w_dec[...])
    pre_s[...] = pre
    hidden = (
        0.5 * pre * (1.0 + jnp.tanh(GELU_SCALE * (pre + GELU_CUBE * pre * pre * pre)))
    ).astype(BF16)
    prediction = state_pad[...] + dot(readout, hidden, ((1,), (1,)))
    pred_own[...] = prediction[:VAR_PAD]
    pred_copy = remote(pred_own, pred_other, pair_sem.at[2], pair_sem.at[3], idx, other)
    pred_copy.start()

    units[0] = jnp.transpose(unit_s[...]).astype(BF16)
    unit_copy = remote(units.at[0], units.at[1], pair_sem.at[0], pair_sem.at[1], idx, other)
    unit_copy.start()

    pre = pre_s[...]
    square = pre * pre
    bend = jnp.tanh(GELU_SCALE * (pre + GELU_CUBE * pre * square))
    slope_s[...] = 0.5 * (1.0 + bend) + 0.5 * pre * (1.0 - bend * bend) * (
        GELU_SCALE * (1.0 + 3.0 * GELU_CUBE * square)
    )

    pred_copy.wait_recv()
    mine = pred_own[...]
    theirs = pred_other[...]
    target = target_pad[...][:VAR_PAD]
    weights = loss_weights[:VAR_PAD]
    miss = mine - target
    miss_other = theirs - target
    apart = mine - theirs
    miss_root = jnp.sqrt(miss * miss + SMOOTH)
    other_root = jnp.sqrt(miss_other * miss_other + SMOOTH)
    apart_root = jnp.sqrt(apart * apart + SMOOTH)
    objective = weights * (
        ((miss_root - SMOOTH_ROOT) + (other_root - SMOOTH_ROOT)) * 0.5
        - (apart_root - SMOOTH_ROOT) * 0.5
    )
    terms = jnp.sum(objective.reshape(VAR_PAD // 8, 8, grid_rows), axis=0)
    folded = terms[:, :128]
    for start in range(128, grid_rows, 128):
        folded = folded + terms[:, start : start + 128]
    loss_own[...] = folded
    loss_all[idx] = folded
    grad_prediction = weights * (miss / miss_root * 0.5 - apart / apart_root * 0.5)
    grad_prediction = jnp.concatenate(
        [grad_prediction, jnp.zeros((READ_PAD - VAR_PAD, grid_rows), F32)], axis=0
    ).astype(BF16)

    grad_hidden = dot(grad_prediction, readout, ((0,), (0,)))
    grad_pre = (grad_hidden * slope_s[...]).astype(BF16)
    gpre_s[0] = grad_pre[:, :half]
    gpre_s[1] = grad_pre[:, half:]
    gpre_copy = remote(
        gpre_s.at[other], gpre_other, pair_sem.at[4], pair_sem.at[5], idx, other
    )
    gpre_copy.start()

    def loss_copy(step):
        goal = lax.rem(idx + step, count)
        return remote(
            loss_own,
            loss_all.at[idx],
            loss_send_sem.at[step],
            loss_recv_sem.at[step],
            goal,
            member,
        )

    def loss_in(step):
        start = lax.rem(idx + count - step, count)
        return remote(
            loss_own,
            loss_all.at[start],
            loss_send_sem.at[step],
            loss_recv_sem.at[step],
            start,
            member,
        )

    for step in range(1, count):
        loss_copy(step).start()

    pre_s[...] = dot(grad_pre, w_dec[...], ((1,), (1,)))

    unit_copy.wait_recv()
    gpre_copy.wait_recv()
    grad_here = jnp.concatenate([gpre_s[member], gpre_other[...]], axis=0)

    def weight_rows(chunk):
        rows = pl.ds(pl.multiple_of(chunk * share_rows, share_rows), share_rows)
        return dot(jnp.concatenate([units[0, rows], units[1, rows]], axis=1), grad_here)

    def y_copy(step):
        return remote(
            y_send.at[step], y_recv.at[step], ys_sem.at[step], yr_sem.at[step], partner, member
        )

    rising = depth - 1 - level
    falls_first = level >= depth // 2

    def target_at(step):
        fall = jnp.where(step < level, step, depth - 1 - (step - level))
        rise = jnp.where(step < rising, depth - 1 - step, step - rising)
        return jnp.where(step == depth - 1, level, jnp.where(falls_first, fall, rise))

    def z_copy(step):
        goal = target_at(step)
        up = goal > level
        hop = jnp.where(up, level + 1, level - 1)
        slot = jnp.where(jnp.logical_not(up) & (hop == goal), depth, goal)
        return remote(
            z_send.at[step],
            z_recv.at[slot],
            zs_sem.at[step],
            zr_sem.at[slot],
            2 * hop + parity,
            member,
        )

    def z_wait(slot):
        remote(
            z_send.at[0], z_recv.at[slot], zs_sem.at[0], zr_sem.at[slot], partner, member
        ).wait_recv()

    def send_partner(step, carry):
        chunk = 2 * target_at(step) + (1 - parity)
        y_send[step] = weight_rows(chunk).astype(BF16)
        y_copy(step).start()
        return carry

    lax.fori_loop(0, depth, send_partner, 0)

    grad_unit = pre_s[...]
    unit = unit_s[...]
    grad_aggregate = inverse * (
        grad_unit
        - jnp.mean(grad_unit, axis=-1, keepdims=True)
        - unit * jnp.mean(grad_unit * unit, axis=-1, keepdims=True)
    )
    rounded = grad_aggregate.astype(BF16)
    tile_grad = (dot(spread_high, rounded) + dot(spread_low, rounded)).astype(BF16)
    grad_send[0] = tile_grad[:slot_rows]
    grad_send[1] = tile_grad[2 * slot_rows :]
    grad_recv[1] = tile_grad[slot_rows : 2 * slot_rows]
    grad_down = remote(
        grad_send.at[0], grad_recv.at[2], grad_sem.at[0], grad_sem.at[1], idx - 1, member
    )
    grad_up = remote(
        grad_send.at[1], grad_recv.at[0], grad_sem.at[2], grad_sem.at[3], idx + 1, member
    )

    @pl.when(has_low)
    def _():
        grad_down.start()

    @pl.when(has_high)
    def _():
        grad_up.start()

    def send_level(step, carry):
        goal = target_at(step)
        share_sum[...] = weight_rows(2 * goal + parity)
        y_copy(step).wait_recv()
        share_sum[...] += y_recv[step].astype(F32)

        @pl.when(((goal > level) & (level > 0)) | ((goal < level) & (level < depth - 1)))
        def _():
            z_wait(goal)
            share_sum[...] += z_recv[goal].astype(F32)

        z_send[step] = share_sum[...].astype(BF16)
        z_copy(step).start()
        return carry

    lax.fori_loop(0, depth - 1, send_level, 0)
    share_sum[...] = weight_rows(idx)
    y_copy(depth - 1).wait_recv()
    share_sum[...] += y_recv[depth - 1].astype(F32)

    @pl.when(has_high)
    def _():
        remote(
            grad_send.at[0], grad_recv.at[2], grad_sem.at[0], grad_sem.at[1], idx + 1, member
        ).wait_recv()

    @pl.when(has_low)
    def _():
        remote(
            grad_send.at[1], grad_recv.at[0], grad_sem.at[2], grad_sem.at[3], idx - 1, member
        ).wait_recv()

    rows_ref[...] = grad_recv[...].reshape(3 * slot_rows, width)

    for step in range(1, count):
        loss_in(step).wait_recv()
    loss_sum = loss_all[0]
    for step in range(1, count):
        loss_sum = loss_sum + loss_all[step]
    loss_ref[0] = jnp.sum(loss_sum) / grid_total

    @pl.when(level > 0)
    def _():
        z_wait(level)
        share_sum[...] += z_recv[level].astype(F32)

    @pl.when(level < depth - 1)
    def _():
        z_wait(depth)
        share_sum[...] += z_recv[depth].astype(F32)

    share_own[...] = share_sum[...].astype(BF16)
    share_copy = remote(share_own, share_other, pair_sem.at[6], pair_sem.at[7], idx, other)
    share_copy.start()
    own_columns = pl.ds(pl.multiple_of(member * half, half), half)
    other_columns = pl.ds(pl.multiple_of(other * half, half), half)
    share_ref[:, own_columns] = share_own[...]
    share_copy.wait_recv()
    share_ref[:, other_columns] = share_other[...]

    for c in range(PIECES):
        halo_copy(c).wait_send()

    @pl.when(has_onward)
    def _():
        for c in range(PIECES):
            pass_copy(c).wait_send()

    @pl.when(has_low)
    def _():
        for part in range(2):
            feat_copies(part)[0].wait_send()
        grad_down.wait_send()

    @pl.when(has_high)
    def _():
        for part in range(2):
            feat_copies(part)[1].wait_send()
        grad_up.wait_send()

    unit_copy.wait_send()
    pred_copy.wait_send()
    gpre_copy.wait_send()
    share_copy.wait_send()
    for step in range(1, count):
        loss_copy(step).wait_send()
    for step in range(depth):
        y_copy(step).wait_send()
    for step in range(depth - 1):
        z_copy(step).wait_send()


def finish(
    pick_hbm, rows_hbm, share_hbm, latent_grad_hbm, decoder_grad_hbm, pick, rows, share, lat, dec, sem
):
    loads = [
        pltpu.make_async_copy(share_hbm, share, sem.at[0]),
        pltpu.make_async_copy(pick_hbm, pick, sem.at[1]),
        pltpu.make_async_copy(rows_hbm, rows, sem.at[2]),
    ]
    for load in loads:
        load.start()
    loads[0].wait()
    dec[...] = share[...].astype(F32)
    store_dec = pltpu.make_async_copy(dec, decoder_grad_hbm, sem.at[3])
    store_dec.start()
    loads[1].wait()
    loads[2].wait()
    lat[...] = dot(pick[...], rows[...], ((0,), (0,)))
    store_lat = pltpu.make_async_copy(lat, latent_grad_hbm.at[0], sem.at[4])
    store_lat.start()
    store_dec.wait()
    store_lat.wait()


def body(
    latent,
    project_in,
    project_out,
    decoder_weight,
    readout_weight,
    variable_weight,
    area_weight,
    current_state,
    target,
    block_table,
    edge_source,
    edge_weight,
):
    count = lax.axis_size("mp")
    width = latent.shape[2]
    half = width // 2
    depth = count // 2
    share_rows = width // count
    grid_rows = edge_source.shape[1]
    slot_rows = SLOTS * BLOCK_ROWS
    hbm = pl.BlockSpec(memory_space=pltpu.MemorySpace.HBM)
    vmem = pl.BlockSpec(memory_space=pltpu.VMEM)
    smem = pl.BlockSpec(memory_space=pltpu.SMEM)
    dma = pltpu.SemaphoreType.DMA
    mean_loss, rows, pick, share = pl.pallas_call(
        functools.partial(kernel, count, float(count * grid_rows)),
        out_shape=(
            jax.ShapeDtypeStruct((1,), F32),
            jax.ShapeDtypeStruct((3 * slot_rows, width), BF16),
            jax.ShapeDtypeStruct((3 * slot_rows, LAT_DEV), BF16),
            jax.ShapeDtypeStruct((share_rows, width), BF16),
        ),
        in_specs=[hbm] * 12,
        out_specs=(smem, vmem, vmem, vmem),
        scratch_shapes=[
            pltpu.VMEM(readout_weight.shape, BF16),
            pltpu.VMEM((1, variable_weight.shape[0]), F32),
            pltpu.VMEM((1, grid_rows), F32),
            pltpu.VMEM(current_state.shape, F32),
            pltpu.VMEM(target.shape, F32),
            pltpu.SMEM((3, SLOTS, count), jnp.int32),
            pltpu.VMEM(edge_source.shape, jnp.int32),
            pltpu.VMEM(edge_weight.shape, F32),
            pltpu.VMEM((3, LAT_DEV, width), BF16),
            pltpu.VMEM((width, 3 * width), BF16),
            pltpu.VMEM((width, width), BF16),
            pltpu.VMEM((width, width), BF16),
            pltpu.VMEM((LAT_DEV, width), BF16),
            pltpu.VMEM((3 * LAT_DEV, width), BF16),
            pltpu.VMEM((3 * LAT_DEV, width), BF16),
            pltpu.VMEM((LAT_DEV, width), BF16),
            pltpu.VMEM((width // 128, 2 * LAT_DEV, 128), F32),
            pltpu.VMEM((width // 128, 2 * LAT_DEV, 128), F32),
            pltpu.VMEM((width // 128, 2 * LAT_DEV, 128), F32),
            pltpu.VMEM((3, slot_rows, width), BF16),
            pltpu.VMEM((3, slot_rows, width), BF16),
            pltpu.VMEM((grid_rows, width), F32),
            pltpu.VMEM((2, width, grid_rows), BF16),
            pltpu.VMEM((grid_rows, width), F32),
            pltpu.VMEM((grid_rows, width), F32),
            pltpu.VMEM((READ_PAD, width), F32),
            pltpu.VMEM((READ_PAD, grid_rows), F32),
            pltpu.VMEM((READ_PAD, grid_rows), F32),
            pltpu.VMEM((8, 128), F32),
            pltpu.VMEM((VAR_PAD, grid_rows), F32),
            pltpu.VMEM((VAR_PAD, grid_rows), F32),
            pltpu.VMEM((8, 128), F32),
            pltpu.VMEM((count, 8, 128), F32),
            pltpu.VMEM((2, grid_rows, half), BF16),
            pltpu.VMEM((grid_rows, half), BF16),
            pltpu.VMEM((2, slot_rows, width), BF16),
            pltpu.VMEM((3, slot_rows, width), BF16),
            pltpu.VMEM((depth, share_rows, half), BF16),
            pltpu.VMEM((depth, share_rows, half), BF16),
            pltpu.VMEM((depth, share_rows, half), BF16),
            pltpu.VMEM((depth + 1, share_rows, half), BF16),
            pltpu.VMEM((share_rows, half), F32),
            pltpu.VMEM((share_rows, half), BF16),
            pltpu.VMEM((share_rows, half), BF16),
            dma((6,)),
            dma((8,)),
            dma((2, PIECES)),
            dma((2, PIECES)),
            dma((4, 2)),
            dma((8,)),
            dma((count,)),
            dma((count,)),
            dma((4,)),
            dma((depth,)),
            dma((depth,)),
            dma((depth,)),
            dma((depth + 1,)),
        ],
        compiler_params=pltpu.CompilerParams(
            collective_id=0, has_side_effects=True, vmem_limit_bytes=62 * 1024 * 1024
        ),
    )(
        latent,
        project_in,
        project_out,
        decoder_weight,
        readout_weight,
        variable_weight.reshape(1, -1),
        area_weight.reshape(1, -1),
        current_state,
        target,
        jnp.transpose(block_table, (1, 2, 0)),
        edge_source,
        edge_weight,
    )
    latent_grad, decoder_grad = pl.pallas_call(
        finish,
        out_shape=(
            jax.ShapeDtypeStruct((1, LAT_DEV, width), F32),
            jax.ShapeDtypeStruct((share_rows, width), F32),
        ),
        in_specs=[hbm] * 3,
        out_specs=(hbm, hbm),
        scratch_shapes=[
            pltpu.VMEM((3 * slot_rows, LAT_DEV), BF16),
            pltpu.VMEM((3 * slot_rows, width), BF16),
            pltpu.VMEM((share_rows, width), BF16),
            pltpu.VMEM((LAT_DEV, width), F32),
            pltpu.VMEM((share_rows, width), F32),
            dma((5,)),
        ],
        compiler_params=pltpu.CompilerParams(vmem_limit_bytes=62 * 1024 * 1024),
    )(pick, rows, share)
    return (mean_loss, latent_grad, decoder_grad)


def solution(mesh):
    in_specs = (
        P("member", ("groups", "mp"), None),
        P(),
        P(),
        P(),
        P(),
        P(),
        P(("groups", "mp")),
        P(None, ("groups", "mp")),
        P(None, ("groups", "mp")),
        P("groups", None, None),
        P(None, ("groups", "mp")),
        P(None, ("groups", "mp")),
    )
    out_specs = (P("groups"), P("member", ("groups", "mp"), None), P(("groups", "mp"), None))
    return jax.shard_map(body, mesh=mesh, in_specs=in_specs, out_specs=out_specs, check_vma=False)
```
